32 devices in a mesh: wn: 4 (over y, core), sp: 8 (over z, x).
Axes of the slice: x: 2, y: 2, z: 4, core: 2. Of those that a mesh axis runs over, the one named last changes fastest.
Arguments:
- random_slabs: float32 [8, 3, 512, 1024], P(None, None, 'wn', 'sp'), may hold values from -6 to 6
- stress: float32 [6, 512], P(None, 'wn'), may hold values from -0.8 to 2, as said below
- profile: float32 [512], P('wn'), may hold values from 0.2 to 1.2
Outputs:
- inflow: float32 [8, 3, 512, 1024], P(None, None, 'wn', 'sp')
The draws below stay inside these ranges and needn't reach their ends.
Inputs may be any that keep to these rules, and one draw needn't show every extreme that they name: R11, R22 and R33 are positive, and each off-diagonal stress is at most 0.4 times the square root of the product of its two diagonal stresses in magnitude.
All inputs are finite; a program needn't handle non-finite values.
Results may differ from the reference program's by a relative error of at most 0.0003.
Values sent between devices are 32-bit elements; how exact they have to be, the bound alone decides.
A program may use at most 128 MiB of HBM per device.

```python
import jax
import jax.numpy as jnp
from jax import lax

STEPS = 8
H = 64
NY = 512
NZ = 1024


carry_over = 0.85


def draw_random_slabs(key, part):
    source = jax.random.truncated_normal(key, -1.7, 1.7, (STEPS, 3, NY + 1, NZ + 1), jnp.float32)
    here = source[:, :, 1:, 1:]
    below = source[:, :, :-1, 1:]
    beside = source[:, :, 1:, :-1]
    corner = source[:, :, :-1, :-1]
    return here - carry_over * below - carry_over * beside + carry_over * carry_over * corner


def draw_stress(key, part):
    diag_key = jax.random.fold_in(key, 11)
    corr_key = jax.random.fold_in(key, 23)
    diagonal = jnp.exp(jax.random.uniform(diag_key, (3, NY), jnp.float32, jnp.log(0.5), jnp.log(2.0)))
    correlation = jax.random.uniform(corr_key, (3, NY), jnp.float32, -0.4, 0.4)
    cross_yx = correlation[0] * jnp.sqrt(diagonal[0] * diagonal[1])
    cross_zx = correlation[1] * jnp.sqrt(diagonal[0] * diagonal[2])
    cross_zy = correlation[2] * jnp.sqrt(diagonal[1] * diagonal[2])
    return jnp.concatenate([diagonal, jnp.stack([cross_yx, cross_zx, cross_zy])], axis=0)


def steps_of(rng, dims, pieces, least, largest):
    def one(position, shards_of):
        steps = jax.random.uniform(jax.random.fold_in(jax.random.fold_in(rng, 6), position), (shards_of,), jnp.float32, least / len(pieces), largest / len(pieces))
        return jnp.repeat(jnp.exp(steps), dims[position] // shards_of).reshape((-1,) + (1,) * (len(dims) - position - 1))

    factor_of = one(*pieces[0])
    for cut in pieces[1:]:
        factor_of = factor_of * one(*cut)
    return factor_of


def setup_inputs(seed: int = 0) -> dict:
    splits = jax.random.split(jax.random.key(seed), 4)
    random_slabs = draw_random_slabs(jax.random.fold_in(splits[3], 71), 0)
    stress = draw_stress(jax.random.fold_in(splits[3], 71), 0)
    profile = jnp.clip(0.2 + 1 * jax.random.uniform(splits[2], (NY,), jnp.float32) ** steps_of(splits[2], (NY,), ((0, 4),), -0.2, 0.2), 0.2, 1.2)
    return dict(random_slabs=random_slabs, stress=stress, profile=profile)


def band_matrix(reach):
    width = 2 * reach
    offset = jnp.arange(-reach, reach + 1).astype(jnp.float32)
    scale_len = reach / 2.0
    norming = jnp.sqrt(jnp.sum(jnp.exp(-jnp.pi * offset * offset / (scale_len * scale_len))))
    source = jnp.arange(2 * width)[:, None]
    target = jnp.arange(width)[None, :]
    lag = (source - target - reach).astype(jnp.float32)
    values = jnp.exp(-jnp.pi * lag * lag / (2.0 * scale_len * scale_len)) / norming
    return jnp.where(jnp.abs(lag) <= reach, values, 0.0).astype(jnp.float32)

def filter_last(padded, reach):
    width = 2 * reach
    band = band_matrix(reach)
    lead = padded.shape[:-1]
    blocks = padded.reshape(lead + (padded.shape[-1] // width, width))
    upper = jnp.matmul(blocks[..., :-1, :], band[:width], precision=lax.Precision.HIGHEST)
    lower = jnp.matmul(blocks[..., 1:, :], band[width:], precision=lax.Precision.HIGHEST)
    return (upper + lower).reshape(lead + (padded.shape[-1] - width,))

def filter_rows(padded, reach):
    width = 2 * reach
    band = band_matrix(reach)
    steps_n, comps, length, cols = padded.shape
    blocks = padded.reshape(steps_n, comps, length // width, width, cols)
    upper = jnp.einsum('scbjz,ji->scbiz', blocks[:, :, :-1], band[:width], precision=lax.Precision.HIGHEST)
    lower = jnp.einsum('scbjz,ji->scbiz', blocks[:, :, 1:], band[width:], precision=lax.Precision.HIGHEST)
    return (upper + lower).reshape(steps_n, comps, length - width, cols)

def lund(scaled, stress, profile):
    chol_xx = jnp.sqrt(stress[0])
    chol_yx = stress[3] / chol_xx
    chol_yy = jnp.sqrt(stress[1] - chol_yx * chol_yx)
    chol_zx = stress[4] / chol_xx
    chol_zy = (stress[5] - chol_yx * chol_zx) / chol_yy
    chol_zz = jnp.sqrt(stress[2] - chol_zx * chol_zx - chol_zy * chol_zy)
    first = profile[:, None] + chol_xx[:, None] * scaled[:, 0]
    second = chol_yx[:, None] * scaled[:, 0] + chol_yy[:, None] * scaled[:, 1]
    third = chol_zx[:, None] * scaled[:, 0] + chol_zy[:, None] * scaled[:, 1] + chol_zz[:, None] * scaled[:, 2]
    return jnp.stack([first, second, third], axis=1)

def reference(random_slabs, stress, profile):
    padded = jnp.pad(random_slabs, ((0, 0), (0, 0), (H, H), (0, 0)))
    normal_pass = filter_rows(padded, H)
    wrapped = jnp.concatenate([normal_pass[..., -H:], normal_pass, normal_pass[..., :H]], axis=-1)
    filtered = filter_last(wrapped, H)
    row_mean = lax.optimization_barrier(jnp.sum(filtered, axis=-1)) / NZ
    centred = filtered - row_mean[..., None]
    row_var = lax.optimization_barrier(jnp.sum(centred * centred, axis=-1)) / NZ
    scaled = centred / jnp.sqrt(row_var[..., None] + 1e-06)
    return lund(scaled, stress, profile)
```

```python
import functools

import jax
import jax.numpy as jnp
from jax import lax
from jax.experimental import pallas as pl
from jax.experimental.pallas import tpu as pltpu
from jax.sharding import PartitionSpec as P

H = 64
LAG = 2

epsilon = 1e-06
MESH = pl.DeviceIdType.MESH
HIGHEST = lax.Precision.HIGHEST


def filter_values(lag, norming):
    scale_len = H / 2.0
    values = jnp.exp(-jnp.pi * lag * lag / (2.0 * scale_len * scale_len)) / norming
    return jnp.where(jnp.abs(lag) <= H, values, 0.0)


def norming_of():
    shape = (-(-(2 * H + 1) // 1024) * 8, 128)
    index = (
        lax.broadcasted_iota(jnp.int32, shape, 0) * 128 + lax.broadcasted_iota(jnp.int32, shape, 1)
    )
    offset = (index - H).astype(jnp.float32)
    scale_len = H / 2.0
    squares = jnp.exp(-jnp.pi * offset * offset / (scale_len * scale_len))
    squares = jnp.where(index <= 2 * H, squares, 0.0)
    return jnp.sqrt(jnp.sum(jnp.sum(squares, axis=1, keepdims=True), axis=0, keepdims=True))


def kernel(
    wn_n, sp_n, x_ref, stress_ref, profile_ref, out_ref,
    padded, normal, to_left, to_right, from_left, from_right, filt, stats, outbuf,
    row_band, span_band, chol,
    load_sem, store_sem, wn_send, wn_recv, sp_send, sp_recv, st_send, st_recv,
):
    steps_n, comps, rows, cols = x_ref.shape
    wn = lax.axis_index("wn")
    me = lax.axis_index("sp")
    left, right = lax.rem(me + sp_n - 1, sp_n), lax.rem(me + 1, sp_n)

    def load(s):
        return pltpu.make_async_copy(
            x_ref.at[s], padded.at[s, :, pl.ds(H, rows)], load_sem.at[s]
        )

    for s in range(steps_n):
        load(s).start()

    barrier = pltpu.get_barrier_semaphore()

    def greet(d, carry):
        pl.semaphore_signal(
            barrier, inc=1, device_id={"sp": lax.rem(me + d, sp_n)}, device_id_type=MESH
        )
        return carry

    lax.fori_loop(1, sp_n, greet, 0)

    @pl.when(wn > 0)
    def _():
        pl.semaphore_signal(barrier, inc=1, device_id={"wn": wn - 1}, device_id_type=MESH)

    @pl.when(wn < wn_n - 1)
    def _():
        pl.semaphore_signal(barrier, inc=1, device_id={"wn": wn + 1}, device_id_type=MESH)

    norming = norming_of()
    target = lax.broadcasted_iota(jnp.int32, (rows, 2 * rows), 0)
    source = lax.broadcasted_iota(jnp.int32, (rows, 2 * rows), 1)
    row_band[...] = filter_values((source - target - H).astype(jnp.float32), norming)
    source = lax.broadcasted_iota(jnp.int32, (2 * cols, cols), 0)
    target = lax.broadcasted_iota(jnp.int32, (2 * cols, cols), 1)
    place = jnp.where(
        source < cols, source, jnp.where(source < cols + H, source - cols - H, source - H)
    )
    span_band[...] = filter_values((place - target).astype(jnp.float32), norming)

    r = [stress_ref[pl.ds(i, 1), :] for i in range(6)]
    a11 = jnp.sqrt(r[0])
    a21 = r[3] / a11
    a22 = jnp.sqrt(r[1] - a21 * a21)
    a31 = r[4] / a11
    a32 = (r[5] - a21 * a31) / a22
    a33 = jnp.sqrt(r[2] - a31 * a31 - a32 * a32)
    for i, a in enumerate((a11, a21, a22, a31, a32, a33, profile_ref[...])):
        chol[pl.ds(i, 1), :] = a

    @pl.when(wn == 0)
    def _():
        padded[:, :, pl.ds(0, H)] = jnp.zeros((steps_n, comps, H, cols), jnp.float32)

    @pl.when(wn == wn_n - 1)
    def _():
        padded[:, :, pl.ds(H + rows, H)] = jnp.zeros((steps_n, comps, H, cols), jnp.float32)

    pl.semaphore_wait(
        barrier, sp_n - 1 + (wn > 0).astype(jnp.int32) + (wn < wn_n - 1).astype(jnp.int32)
    )

    def rows_down(s):
        return pltpu.make_async_remote_copy(
            src_ref=x_ref.at[s, :, pl.ds(0, H)],
            dst_ref=padded.at[s, :, pl.ds(H + rows, H)],
            send_sem=wn_send.at[0, s], recv_sem=wn_recv.at[0, s],
            device_id={"wn": wn - 1}, device_id_type=MESH,
        )

    def rows_up(s):
        return pltpu.make_async_remote_copy(
            src_ref=x_ref.at[s, :, pl.ds(rows - H, H)],
            dst_ref=padded.at[s, :, pl.ds(0, H)],
            send_sem=wn_send.at[1, s], recv_sem=wn_recv.at[1, s],
            device_id={"wn": wn + 1}, device_id_type=MESH,
        )

    def send_rows(s, carry):
        @pl.when(wn > 0)
        def _():
            rows_down(s).start()

        @pl.when(wn < wn_n - 1)
        def _():
            rows_up(s).start()

        return carry

    lax.fori_loop(0, steps_n, send_rows, 0)

    def cols_left(s):
        return pltpu.make_async_remote_copy(
            src_ref=to_left.at[s], dst_ref=from_right.at[s],
            send_sem=sp_send.at[0, s], recv_sem=sp_recv.at[0, s],
            device_id={"sp": left}, device_id_type=MESH,
        )

    def cols_right(s):
        return pltpu.make_async_remote_copy(
            src_ref=to_right.at[s], dst_ref=from_left.at[s],
            send_sem=sp_send.at[1, s], recv_sem=sp_recv.at[1, s],
            device_id={"sp": right}, device_id_type=MESH,
        )

    low_lanes = lax.broadcasted_iota(jnp.int32, (H, cols), 1) < H

    def row_phase(s, carry):
        load(s).wait()

        @pl.when(wn < wn_n - 1)
        def _():
            rows_down(s).wait_recv()

        @pl.when(wn > 0)
        def _():
            rows_up(s).wait_recv()

        for c in range(comps):
            done = jnp.dot(
                row_band[...], padded[s, c], precision=HIGHEST,
                preferred_element_type=jnp.float32,
            )
            normal[s, c] = done
            top, bottom = done[:H], done[H:]
            to_left[s, c] = jnp.where(low_lanes, top, pltpu.roll(bottom, H, 1))
            to_right[s, c] = jnp.where(low_lanes, pltpu.roll(top, H, 1), bottom)
        cols_left(s).start()
        cols_right(s).start()
        return carry

    lax.fori_loop(0, steps_n, row_phase, 0)

    def stats_copy(s, d):
        return pltpu.make_async_remote_copy(
            src_ref=stats.at[s, me], dst_ref=stats.at[s, me],
            send_sem=st_send.at[s, d], recv_sem=st_recv.at[s, d],
            device_id={"sp": lax.rem(me + d, sp_n)}, device_id_type=MESH,
        )

    lane = lax.broadcasted_iota(jnp.int32, (rows, cols), 1)

    def span_phase(s):
        cols_left(s).wait_recv()
        cols_right(s).wait_recv()
        packed = jnp.zeros((rows, cols), jnp.float32)
        for c in range(comps):
            lows, highs = from_left[s, c], from_right[s, c]
            halo = jnp.concatenate(
                [
                    jnp.where(low_lanes, lows, pltpu.roll(highs, H, 1)),
                    jnp.where(low_lanes, pltpu.roll(lows, H, 1), highs),
                ],
                axis=0,
            )
            done = jnp.dot(
                jnp.concatenate([normal[s, c], halo], axis=1), span_band[...],
                precision=HIGHEST, preferred_element_type=jnp.float32,
            )
            filt[s, c] = done
            mean = jnp.sum(done, axis=1, keepdims=True) / cols
            away = done - mean
            second = jnp.sum(away * away, axis=1, keepdims=True)
            packed = jnp.where(lane == c, mean, packed)
            packed = jnp.where(lane == comps + c, second, packed)
        stats[s, me] = packed.T[:8]

        def send(d, carry):
            stats_copy(s, d).start()
            return carry

        lax.fori_loop(1, sp_n, send, 0)

    def store(s):
        return pltpu.make_async_copy(outbuf.at[s], out_ref.at[s], store_sem.at[s])

    def last_phase(s):
        def receive(d, carry):
            stats_copy(s, d).wait_recv()
            return carry

        lax.fori_loop(1, sp_n, receive, 0)
        parts = stats[s]
        total = jnp.sum(parts, axis=0) / sp_n
        away = parts - total[None]
        between = jnp.sum(away * away, axis=0) / sp_n
        var = total[comps : 2 * comps] / cols + between[:comps]
        inv = 1.0 / jnp.sqrt(var + epsilon)
        mean = total[:comps]
        i0, i1, i2 = inv[0:1], inv[1:2], inv[2:3]
        a = [chol[pl.ds(i, 1), :] for i in range(7)]
        table = [
            mean[0:1], mean[1:2], mean[2:3],
            a[0] * i0, a[1] * i0, a[2] * i1, a[3] * i0, a[4] * i1, a[5] * i2, a[6],
        ]
        sub = lax.broadcasted_iota(jnp.int32, (16, rows), 0)
        stacked = jnp.zeros((16, rows), jnp.float32)
        for k, v in enumerate(table):
            stacked = jnp.where(sub == k, v, stacked)
        turned = jnp.concatenate([stacked, jnp.zeros((rows - 16, rows), jnp.float32)], axis=0).T
        col = [turned[:, k : k + 1] for k in range(len(table))]
        d0 = filt[s, 0] - col[0]
        d1 = filt[s, 1] - col[1]
        d2 = filt[s, 2] - col[2]
        outbuf[s, 0] = col[9] + col[3] * d0
        outbuf[s, 1] = col[4] * d0 + col[5] * d1
        outbuf[s, 2] = col[6] * d0 + col[7] * d1 + col[8] * d2
        store(s).start()

    def both(s, carry):
        @pl.when(s < steps_n)
        def _():
            span_phase(s)

        @pl.when(s >= LAG)
        def _():
            last_phase(s - LAG)

        return carry

    lax.fori_loop(0, steps_n + LAG, both, 0)

    def finish(s, carry):
        @pl.when(wn > 0)
        def _():
            rows_down(s).wait_send()

        @pl.when(wn < wn_n - 1)
        def _():
            rows_up(s).wait_send()

        cols_left(s).wait_send()
        cols_right(s).wait_send()

        def sent(d, inner):
            stats_copy(s, d).wait_send()
            return inner

        lax.fori_loop(1, sp_n, sent, 0)
        store(s).wait()
        return carry

    lax.fori_loop(0, steps_n, finish, 0)


def body(random_slabs, stress, profile):
    steps_n, comps, rows, cols = random_slabs.shape
    assert rows == 2 * H and cols == 2 * H and comps == 3
    wn_n, sp_n = lax.axis_size("wn"), lax.axis_size("sp")
    f32 = jnp.float32
    half = (steps_n, comps, H, cols)
    return pl.pallas_call(
        functools.partial(kernel, wn_n, sp_n),
        out_shape=jax.ShapeDtypeStruct(random_slabs.shape, f32),
        in_specs=[
            pl.BlockSpec(memory_space=pl.ANY),
            pl.BlockSpec(memory_space=pltpu.VMEM),
            pl.BlockSpec(memory_space=pltpu.VMEM),
        ],
        out_specs=pl.BlockSpec(memory_space=pl.ANY),
        scratch_shapes=[
            pltpu.VMEM((steps_n, comps, 2 * rows, cols), f32),
            pltpu.VMEM((steps_n, comps, rows, cols), f32),
            pltpu.VMEM(half, f32),
            pltpu.VMEM(half, f32),
            pltpu.VMEM(half, f32),
            pltpu.VMEM(half, f32),
            pltpu.VMEM((steps_n, comps, rows, cols), f32),
            pltpu.VMEM((steps_n, sp_n, 8, rows), f32),
            pltpu.VMEM((steps_n, comps, rows, cols), f32),
            pltpu.VMEM((rows, 2 * rows), f32),
            pltpu.VMEM((2 * cols, cols), f32),
            pltpu.VMEM((8, rows), f32),
            pltpu.SemaphoreType.DMA((steps_n,)),
            pltpu.SemaphoreType.DMA((steps_n,)),
            pltpu.SemaphoreType.DMA((2, steps_n)),
            pltpu.SemaphoreType.DMA((2, steps_n)),
            pltpu.SemaphoreType.DMA((2, steps_n)),
            pltpu.SemaphoreType.DMA((2, steps_n)),
            pltpu.SemaphoreType.DMA((steps_n, sp_n)),
            pltpu.SemaphoreType.DMA((steps_n, sp_n)),
        ],
        compiler_params=pltpu.CompilerParams(
            collective_id=0, has_side_effects=True, vmem_limit_bytes=40 * 2**20
        ),
    )(random_slabs, stress, profile.reshape(1, rows))


def solution(mesh):
    return jax.shard_map(
        body,
        mesh=mesh,
        in_specs=(P(None, None, "wn", "sp"), P(None, "wn"), P("wn")),
        out_specs=P(None, None, "wn", "sp"),
        check_vma=False,
    )
```

```python
import functools

import jax
import jax.numpy as jnp
from jax import lax
from jax.experimental import pallas as pl
from jax.experimental.pallas import tpu as pltpu
from jax.sharding import PartitionSpec as P

H = 64
FIRST = 2
LAG = 2

epsilon = 1e-06
MESH = pl.DeviceIdType.MESH
HIGHEST = lax.Precision.HIGHEST


def filter_values(lag, norming):
    scale_len = H / 2.0
    values = jnp.exp(-jnp.pi * lag * lag / (2.0 * scale_len * scale_len)) / norming
    return jnp.where(jnp.abs(lag) <= H, values, 0.0)


def norming_of():
    shape = (-(-(2 * H + 1) // 1024) * 8, 128)
    index = (
        lax.broadcasted_iota(jnp.int32, shape, 0) * 128 + lax.broadcasted_iota(jnp.int32, shape, 1)
    )
    offset = (index - H).astype(jnp.float32)
    scale_len = H / 2.0
    squares = jnp.exp(-jnp.pi * offset * offset / (scale_len * scale_len))
    squares = jnp.where(index <= 2 * H, squares, 0.0)
    return jnp.sqrt(jnp.sum(jnp.sum(squares, axis=1, keepdims=True), axis=0, keepdims=True))


def kernel(
    wn_n, sp_n, x_ref, stress_hbm, profile_hbm, out_ref,
    stress_ref, profile_ref, padded, normal, to_left, to_right, from_left, from_right, filt, stats, outbuf,
    row_band, span_band, chol,
    load_sem, small_sem, store_sem, wn_send, wn_recv, sp_send, sp_recv, st_send, st_recv,
):
    steps_n, comps, rows, cols = x_ref.shape
    wn = lax.axis_index("wn")
    me = lax.axis_index("sp")
    left, right = lax.rem(me + sp_n - 1, sp_n), lax.rem(me + 1, sp_n)

    barrier = pltpu.get_barrier_semaphore()

    def greet(d, carry):
        pl.semaphore_signal(
            barrier, inc=1, device_id={"sp": lax.rem(me + d, sp_n)}, device_id_type=MESH
        )
        return carry

    def load(s):
        return pltpu.make_async_copy(
            x_ref.at[s], padded.at[s, :, pl.ds(H, rows)], load_sem.at[s]
        )

    for s in range(steps_n):
        load(s).start()
    smalls = [
        pltpu.make_async_copy(stress_hbm, stress_ref, small_sem.at[0]),
        pltpu.make_async_copy(profile_hbm, profile_ref, small_sem.at[1]),
    ]
    for small in smalls:
        small.start()

    lax.fori_loop(1, sp_n, greet, 0)

    @pl.when(wn > 0)
    def _():
        pl.semaphore_signal(barrier, inc=1, device_id={"wn": wn - 1}, device_id_type=MESH)

    @pl.when(wn < wn_n - 1)
    def _():
        pl.semaphore_signal(barrier, inc=1, device_id={"wn": wn + 1}, device_id_type=MESH)

    low_lanes = lax.broadcasted_iota(jnp.int32, (H, cols), 1) < H

    def pack(s, c, tile):
        top, bottom = tile[:H], tile[H:]
        to_left[s, c] = jnp.where(low_lanes, top, pltpu.roll(bottom, H, 1))
        to_right[s, c] = jnp.where(low_lanes, pltpu.roll(top, H, 1), bottom)

    def halo_of(s, c):
        lows, highs = from_left[s, c], from_right[s, c]
        return jnp.concatenate(
            [
                jnp.where(low_lanes, lows, pltpu.roll(highs, H, 1)),
                jnp.where(low_lanes, pltpu.roll(lows, H, 1), highs),
            ],
            axis=0,
        )

    for s in range(FIRST):
        load(s).wait()
        for c in range(comps):
            pack(s, c, padded[s, c, pl.ds(H, rows)])

    pl.semaphore_wait(
        barrier, sp_n - 1 + (wn > 0).astype(jnp.int32) + (wn < wn_n - 1).astype(jnp.int32)
    )

    def cols_left(s):
        return pltpu.make_async_remote_copy(
            src_ref=to_left.at[s], dst_ref=from_right.at[s],
            send_sem=sp_send.at[0, s], recv_sem=sp_recv.at[0, s],
            device_id={"sp": left}, device_id_type=MESH,
        )

    def cols_right(s):
        return pltpu.make_async_remote_copy(
            src_ref=to_right.at[s], dst_ref=from_left.at[s],
            send_sem=sp_send.at[1, s], recv_sem=sp_recv.at[1, s],
            device_id={"sp": right}, device_id_type=MESH,
        )

    for s in range(FIRST):
        cols_left(s).start()
        cols_right(s).start()

    def rows_down(s, filtered=False):
        return pltpu.make_async_remote_copy(
            src_ref=padded.at[s, :, pl.ds(H, H)] if filtered else x_ref.at[s, :, pl.ds(0, H)],
            dst_ref=padded.at[s, :, pl.ds(H + rows, H)],
            send_sem=wn_send.at[0, s], recv_sem=wn_recv.at[0, s],
            device_id={"wn": wn - 1}, device_id_type=MESH,
        )

    def rows_up(s, filtered=False):
        return pltpu.make_async_remote_copy(
            src_ref=padded.at[s, :, pl.ds(rows, H)]
            if filtered
            else x_ref.at[s, :, pl.ds(rows - H, H)],
            dst_ref=padded.at[s, :, pl.ds(0, H)],
            send_sem=wn_send.at[1, s], recv_sem=wn_recv.at[1, s],
            device_id={"wn": wn + 1}, device_id_type=MESH,
        )

    def send_rows(s, filtered):
        @pl.when(wn > 0)
        def _():
            rows_down(s, filtered).start()

        @pl.when(wn < wn_n - 1)
        def _():
            rows_up(s, filtered).start()

    def receive_rows(s):
        @pl.when(wn < wn_n - 1)
        def _():
            rows_down(s).wait_recv()

        @pl.when(wn > 0)
        def _():
            rows_up(s).wait_recv()

    def send_later_rows(s, carry):
        send_rows(s, False)
        return carry

    lax.fori_loop(FIRST, steps_n, send_later_rows, 0)

    norming = norming_of()
    target = lax.broadcasted_iota(jnp.int32, (rows, 2 * rows), 0)
    source = lax.broadcasted_iota(jnp.int32, (rows, 2 * rows), 1)
    row_band[...] = filter_values((source - target - H).astype(jnp.float32), norming)
    source = lax.broadcasted_iota(jnp.int32, (2 * cols, cols), 0)
    target = lax.broadcasted_iota(jnp.int32, (2 * cols, cols), 1)
    place = jnp.where(
        source < cols, source, jnp.where(source < cols + H, source - cols - H, source - H)
    )
    span_band[...] = filter_values((place - target).astype(jnp.float32), norming)

    @pl.when(wn == 0)
    def _():
        padded[:, :, pl.ds(0, H)] = jnp.zeros((steps_n, comps, H, cols), jnp.float32)

    @pl.when(wn == wn_n - 1)
    def _():
        padded[:, :, pl.ds(H + rows, H)] = jnp.zeros((steps_n, comps, H, cols), jnp.float32)

    def filter_rows(s, c):
        return jnp.dot(
            row_band[...], padded[s, c], precision=HIGHEST, preferred_element_type=jnp.float32
        )

    def filter_cols(tile, halo):
        return jnp.dot(
            jnp.concatenate([tile, halo], axis=1), span_band[...],
            precision=HIGHEST, preferred_element_type=jnp.float32,
        )

    def row_phase(s, carry):
        load(s).wait()
        receive_rows(s)
        for c in range(comps):
            done = filter_rows(s, c)
            normal[s, c] = done
            pack(s, c, done)
        cols_left(s).start()
        cols_right(s).start()
        return carry

    lax.fori_loop(FIRST, steps_n, row_phase, 0)

    def first_span_phase(s, carry):
        cols_left(s).wait_recv()
        cols_right(s).wait_recv()
        for c in range(comps):
            padded[s, c, pl.ds(H, rows)] = filter_cols(
                padded[s, c, pl.ds(H, rows)], halo_of(s, c)
            )
        send_rows(s, True)
        return carry

    lax.fori_loop(0, FIRST, first_span_phase, 0)

    for small in smalls:
        small.wait()
    r = [stress_ref[pl.ds(i, 1), :] for i in range(6)]
    a11 = jnp.sqrt(r[0])
    a21 = r[3] / a11
    a22 = jnp.sqrt(r[1] - a21 * a21)
    a31 = r[4] / a11
    a32 = (r[5] - a21 * a31) / a22
    a33 = jnp.sqrt(r[2] - a31 * a31 - a32 * a32)
    for i, a in enumerate((a11, a21, a22, a31, a32, a33, profile_ref[...])):
        chol[pl.ds(i, 1), :] = a

    def stats_copy(s, d):
        return pltpu.make_async_remote_copy(
            src_ref=stats.at[s, me], dst_ref=stats.at[s, me],
            send_sem=st_send.at[s, d], recv_sem=st_recv.at[s, d],
            device_id={"sp": lax.rem(me + d, sp_n)}, device_id_type=MESH,
        )

    lane = lax.broadcasted_iota(jnp.int32, (rows, cols), 1)

    def publish(s, tile_of):
        packed = jnp.zeros((rows, cols), jnp.float32)
        for c in range(comps):
            done = tile_of(c)
            filt[s, c] = done
            mean = jnp.sum(done, axis=1, keepdims=True) / cols
            away = done - mean
            second = jnp.sum(away * away, axis=1, keepdims=True)
            packed = jnp.where(lane == c, mean, packed)
            packed = jnp.where(lane == comps + c, second, packed)
        stats[s, me] = packed.T[:8]

        def send(d, carry):
            stats_copy(s, d).start()
            return carry

        lax.fori_loop(1, sp_n, send, 0)

    def span_phase(s):
        cols_left(s).wait_recv()
        cols_right(s).wait_recv()
        publish(s, lambda c: filter_cols(normal[s, c], halo_of(s, c)))

    def first_row_phase(s):
        receive_rows(s)
        publish(s, lambda c: filter_rows(s, c))

    def store(s):
        return pltpu.make_async_copy(outbuf.at[s], out_ref.at[s], store_sem.at[s])

    def last_phase(s):
        def receive(d, carry):
            stats_copy(s, d).wait_recv()
            return carry

        lax.fori_loop(1, sp_n, receive, 0)
        parts = stats[s]
        total = jnp.sum(parts, axis=0) / sp_n
        away = parts - total[None]
        between = jnp.sum(away * away, axis=0) / sp_n
        var = total[comps : 2 * comps] / cols + between[:comps]
        inv = 1.0 / jnp.sqrt(var + epsilon)
        mean = total[:comps]
        i0, i1, i2 = inv[0:1], inv[1:2], inv[2:3]
        a = [chol[pl.ds(i, 1), :] for i in range(7)]
        table = [
            mean[0:1], mean[1:2], mean[2:3],
            a[0] * i0, a[1] * i0, a[2] * i1, a[3] * i0, a[4] * i1, a[5] * i2, a[6],
        ]
        sub = lax.broadcasted_iota(jnp.int32, (16, rows), 0)
        stacked = jnp.zeros((16, rows), jnp.float32)
        for k, v in enumerate(table):
            stacked = jnp.where(sub == k, v, stacked)
        turned = jnp.concatenate([stacked, jnp.zeros((rows - 16, rows), jnp.float32)], axis=0).T
        col = [turned[:, k : k + 1] for k in range(len(table))]
        d0 = filt[s, 0] - col[0]
        d1 = filt[s, 1] - col[1]
        d2 = filt[s, 2] - col[2]
        outbuf[s, 0] = col[9] + col[3] * d0
        outbuf[s, 1] = col[4] * d0 + col[5] * d1
        outbuf[s, 2] = col[6] * d0 + col[7] * d1 + col[8] * d2
        store(s).start()

    def both(s, carry):
        @pl.when(s < steps_n)
        def _():
            span_phase(s)

        @pl.when(s < 2 * FIRST)
        def _():
            first_row_phase(s - FIRST)

        @pl.when(s >= FIRST + LAG)
        def _():
            last_phase(s - LAG)

        @pl.when((s >= FIRST + LAG) & (s < 2 * FIRST + LAG))
        def _():
            last_phase(s - FIRST - LAG)

        return carry

    lax.fori_loop(FIRST, steps_n + LAG, both, 0)

    def finish(s, carry):
        @pl.when(wn > 0)
        def _():
            rows_down(s).wait_send()

        @pl.when(wn < wn_n - 1)
        def _():
            rows_up(s).wait_send()

        cols_left(s).wait_send()
        cols_right(s).wait_send()

        def sent(d, inner):
            stats_copy(s, d).wait_send()
            return inner

        lax.fori_loop(1, sp_n, sent, 0)
        store(s).wait()
        return carry

    lax.fori_loop(0, steps_n, finish, 0)


def body(random_slabs, stress, profile):
    steps_n, comps, rows, cols = random_slabs.shape
    assert rows == 2 * H and cols == 2 * H and comps == 3
    wn_n, sp_n = lax.axis_size("wn"), lax.axis_size("sp")
    f32 = jnp.float32
    half = (steps_n, comps, H, cols)
    return pl.pallas_call(
        functools.partial(kernel, wn_n, sp_n),
        out_shape=jax.ShapeDtypeStruct(random_slabs.shape, f32),
        in_specs=[pl.BlockSpec(memory_space=pltpu.HBM)] * 3,
        out_specs=pl.BlockSpec(memory_space=pl.ANY),
        scratch_shapes=[
            pltpu.VMEM((6, rows), f32),
            pltpu.VMEM((1, rows), f32),
            pltpu.VMEM((steps_n, comps, 2 * rows, cols), f32),
            pltpu.VMEM((steps_n, comps, rows, cols), f32),
            pltpu.VMEM(half, f32),
            pltpu.VMEM(half, f32),
            pltpu.VMEM(half, f32),
            pltpu.VMEM(half, f32),
            pltpu.VMEM((steps_n, comps, rows, cols), f32),
            pltpu.VMEM((steps_n, sp_n, 8, rows), f32),
            pltpu.VMEM((steps_n, comps, rows, cols), f32),
            pltpu.VMEM((rows, 2 * rows), f32),
            pltpu.VMEM((2 * cols, cols), f32),
            pltpu.VMEM((8, rows), f32),
            pltpu.SemaphoreType.DMA((steps_n,)),
            pltpu.SemaphoreType.DMA((2,)),
            pltpu.SemaphoreType.DMA((steps_n,)),
            pltpu.SemaphoreType.DMA((2, steps_n)),
            pltpu.SemaphoreType.DMA((2, steps_n)),
            pltpu.SemaphoreType.DMA((2, steps_n)),
            pltpu.SemaphoreType.DMA((2, steps_n)),
            pltpu.SemaphoreType.DMA((steps_n, sp_n)),
            pltpu.SemaphoreType.DMA((steps_n, sp_n)),
        ],
        compiler_params=pltpu.CompilerParams(
            collective_id=0, has_side_effects=True, vmem_limit_bytes=58 * 2**20
        ),
    )(random_slabs, stress, profile.reshape(1, rows))


def solution(mesh):
    return jax.shard_map(
        body,
        mesh=mesh,
        in_specs=(P(None, None, "wn", "sp"), P(None, "wn"), P("wn")),
        out_specs=P(None, None, "wn", "sp"),
        check_vma=False,
    )
```

```python
import functools

import jax
import jax.numpy as jnp
from jax import lax
from jax.experimental import pallas as pl
from jax.experimental.pallas import tpu as pltpu
from jax.sharding import PartitionSpec as P

H = 64
FIRST = 3
LAG = 4

epsilon = 1e-06
MESH = pl.DeviceIdType.MESH
HIGHEST = lax.Precision.HIGHEST


def filter_values(lag, norming):
    scale_len = H / 2.0
    values = jnp.exp(-jnp.pi * lag * lag / (2.0 * scale_len * scale_len)) / norming
    return jnp.where(jnp.abs(lag) <= H, values, 0.0)


def norming_of():
    shape = (-(-(2 * H + 1) // 1024) * 8, 128)
    index = (
        lax.broadcasted_iota(jnp.int32, shape, 0) * 128 + lax.broadcasted_iota(jnp.int32, shape, 1)
    )
    offset = (index - H).astype(jnp.float32)
    scale_len = H / 2.0
    squares = jnp.exp(-jnp.pi * offset * offset / (scale_len * scale_len))
    squares = jnp.where(index <= 2 * H, squares, 0.0)
    return jnp.sqrt(jnp.sum(jnp.sum(squares, axis=1, keepdims=True), axis=0, keepdims=True))


def kernel(
    wn_n, sp_n, x_ref, stress_hbm, profile_hbm, out_ref,
    stress_ref, profile_ref, padded, normal, to_left, to_right, from_left, from_right, filt, stats, outbuf,
    row_band, span_band, chol,
    load_sem, small_sem, store_sem, wn_send, wn_recv, sp_send, sp_recv, st_send, st_recv,
):
    steps_n, comps, rows, cols = x_ref.shape
    wn = lax.axis_index("wn")
    me = lax.axis_index("sp")
    left, right = lax.rem(me + sp_n - 1, sp_n), lax.rem(me + 1, sp_n)

    barrier = pltpu.get_barrier_semaphore()

    def greet(d, carry):
        pl.semaphore_signal(
            barrier, inc=1, device_id={"sp": lax.rem(me + d, sp_n)}, device_id_type=MESH
        )
        return carry

    def load(s):
        return pltpu.make_async_copy(
            x_ref.at[s], padded.at[s, :, pl.ds(H, rows)], load_sem.at[s]
        )

    for s in range(steps_n):
        load(s).start()
    smalls = [
        pltpu.make_async_copy(stress_hbm, stress_ref, small_sem.at[0]),
        pltpu.make_async_copy(profile_hbm, profile_ref, small_sem.at[1]),
    ]
    for small in smalls:
        small.start()

    lax.fori_loop(1, sp_n, greet, 0)

    @pl.when(wn > 0)
    def _():
        pl.semaphore_signal(barrier, inc=1, device_id={"wn": wn - 1}, device_id_type=MESH)

    @pl.when(wn < wn_n - 1)
    def _():
        pl.semaphore_signal(barrier, inc=1, device_id={"wn": wn + 1}, device_id_type=MESH)

    low_lanes = lax.broadcasted_iota(jnp.int32, (H, cols), 1) < H

    def pack(s, c, tile):
        top, bottom = tile[:H], tile[H:]
        to_left[s, c] = jnp.where(low_lanes, top, pltpu.roll(bottom, H, 1))
        to_right[s, c] = jnp.where(low_lanes, pltpu.roll(top, H, 1), bottom)

    def halo_of(s, c):
        lows, highs = from_left[s, c], from_right[s, c]
        return jnp.concatenate(
            [
                jnp.where(low_lanes, lows, pltpu.roll(highs, H, 1)),
                jnp.where(low_lanes, pltpu.roll(lows, H, 1), highs),
            ],
            axis=0,
        )

    for s in range(FIRST):
        load(s).wait()
        for c in range(comps):
            pack(s, c, padded[s, c, pl.ds(H, rows)])

    pl.semaphore_wait(
        barrier, sp_n - 1 + (wn > 0).astype(jnp.int32) + (wn < wn_n - 1).astype(jnp.int32)
    )

    def cols_left(s):
        return pltpu.make_async_remote_copy(
            src_ref=to_left.at[s], dst_ref=from_right.at[s],
            send_sem=sp_send.at[0, s], recv_sem=sp_recv.at[0, s],
            device_id={"sp": left}, device_id_type=MESH,
        )

    def cols_right(s):
        return pltpu.make_async_remote_copy(
            src_ref=to_right.at[s], dst_ref=from_left.at[s],
            send_sem=sp_send.at[1, s], recv_sem=sp_recv.at[1, s],
            device_id={"sp": right}, device_id_type=MESH,
        )

    for s in range(FIRST):
        cols_left(s).start()
        cols_right(s).start()

    def rows_down(s, filtered=False):
        return pltpu.make_async_remote_copy(
            src_ref=padded.at[s, :, pl.ds(H, H)] if filtered else x_ref.at[s, :, pl.ds(0, H)],
            dst_ref=padded.at[s, :, pl.ds(H + rows, H)],
            send_sem=wn_send.at[0, s], recv_sem=wn_recv.at[0, s],
            device_id={"wn": wn - 1}, device_id_type=MESH,
        )

    def rows_up(s, filtered=False):
        return pltpu.make_async_remote_copy(
            src_ref=padded.at[s, :, pl.ds(rows, H)]
            if filtered
            else x_ref.at[s, :, pl.ds(rows - H, H)],
            dst_ref=padded.at[s, :, pl.ds(0, H)],
            send_sem=wn_send.at[1, s], recv_sem=wn_recv.at[1, s],
            device_id={"wn": wn + 1}, device_id_type=MESH,
        )

    def send_rows(s, filtered):
        @pl.when(wn > 0)
        def _():
            rows_down(s, filtered).start()

        @pl.when(wn < wn_n - 1)
        def _():
            rows_up(s, filtered).start()

    def receive_rows(s):
        @pl.when(wn < wn_n - 1)
        def _():
            rows_down(s).wait_recv()

        @pl.when(wn > 0)
        def _():
            rows_up(s).wait_recv()

    def send_later_rows(s, carry):
        send_rows(s, False)
        return carry

    lax.fori_loop(FIRST, steps_n, send_later_rows, 0)

    norming = norming_of()
    target = lax.broadcasted_iota(jnp.int32, (rows, 2 * rows), 0)
    source = lax.broadcasted_iota(jnp.int32, (rows, 2 * rows), 1)
    row_band[...] = filter_values((source - target - H).astype(jnp.float32), norming)
    source = lax.broadcasted_iota(jnp.int32, (2 * cols, cols), 0)
    target = lax.broadcasted_iota(jnp.int32, (2 * cols, cols), 1)
    place = jnp.where(
        source < cols, source, jnp.where(source < cols + H, source - cols - H, source - H)
    )
    span_band[...] = filter_values((place - target).astype(jnp.float32), norming)

    @pl.when(wn == 0)
    def _():
        padded[:, :, pl.ds(0, H)] = jnp.zeros((steps_n, comps, H, cols), jnp.float32)

    @pl.when(wn == wn_n - 1)
    def _():
        padded[:, :, pl.ds(H + rows, H)] = jnp.zeros((steps_n, comps, H, cols), jnp.float32)

    def filter_rows(s, c):
        return jnp.dot(
            row_band[...], padded[s, c], precision=HIGHEST, preferred_element_type=jnp.float32
        )

    def filter_cols(tile, halo):
        return jnp.dot(
            jnp.concatenate([tile, halo], axis=1), span_band[...],
            precision=HIGHEST, preferred_element_type=jnp.float32,
        )

    def row_phase(s, carry):
        load(s).wait()
        receive_rows(s)
        for c in range(comps):
            done = filter_rows(s, c)
            normal[s, c] = done
            pack(s, c, done)
        cols_left(s).start()
        cols_right(s).start()
        return carry

    lax.fori_loop(FIRST, steps_n, row_phase, 0)

    def first_span_phase(s, carry):
        cols_left(s).wait_recv()
        cols_right(s).wait_recv()
        for c in range(comps):
            padded[s, c, pl.ds(H, rows)] = filter_cols(
                padded[s, c, pl.ds(H, rows)], halo_of(s, c)
            )
        send_rows(s, True)
        return carry

    lax.fori_loop(0, FIRST, first_span_phase, 0)

    for small in smalls:
        small.wait()
    r = [stress_ref[pl.ds(i, 1), :] for i in range(6)]
    a11 = jnp.sqrt(r[0])
    a21 = r[3] / a11
    a22 = jnp.sqrt(r[1] - a21 * a21)
    a31 = r[4] / a11
    a32 = (r[5] - a21 * a31) / a22
    a33 = jnp.sqrt(r[2] - a31 * a31 - a32 * a32)
    for i, a in enumerate((a11, a21, a22, a31, a32, a33, profile_ref[...])):
        chol[pl.ds(i, 1), :] = a

    def stats_copy(s, d):
        return pltpu.make_async_remote_copy(
            src_ref=stats.at[s, me, pl.ds(0, 2 * comps)],
            dst_ref=stats.at[s, me, pl.ds(0, 2 * comps)],
            send_sem=st_send.at[s, d], recv_sem=st_recv.at[s, d],
            device_id={"sp": lax.rem(me + d, sp_n)}, device_id_type=MESH,
        )

    lane = lax.broadcasted_iota(jnp.int32, (rows, cols), 1)

    def publish(s, tile_of):
        packed = jnp.zeros((rows, cols), jnp.float32)
        for c in range(comps):
            done = tile_of(c)
            filt[s, c] = done
            mean = jnp.sum(done, axis=1, keepdims=True) / cols
            away = done - mean
            second = jnp.sum(away * away, axis=1, keepdims=True)
            packed = jnp.where(lane == c, mean, packed)
            packed = jnp.where(lane == comps + c, second, packed)
        stats[s, me, pl.ds(0, 2 * comps)] = packed.T[: 2 * comps]

        def send(d, carry):
            stats_copy(s, d).start()
            return carry

        lax.fori_loop(1, sp_n, send, 0)

    def span_phase(s):
        cols_left(s).wait_recv()
        cols_right(s).wait_recv()
        publish(s, lambda c: filter_cols(normal[s, c], halo_of(s, c)))

    def first_row_phase(s):
        receive_rows(s)
        publish(s, lambda c: filter_rows(s, c))

    def store(s):
        return pltpu.make_async_copy(outbuf.at[s], out_ref.at[s], store_sem.at[s])

    def last_phase(s):
        @pl.when(wn > 0)
        def _():
            rows_down(s).wait_send()

        @pl.when(wn < wn_n - 1)
        def _():
            rows_up(s).wait_send()

        cols_left(s).wait_send()
        cols_right(s).wait_send()

        def sent(d, inner):
            stats_copy(s, d).wait_send()
            return inner

        lax.fori_loop(1, sp_n, sent, 0)

        def receive(d, carry):
            stats_copy(s, d).wait_recv()
            return carry

        lax.fori_loop(1, sp_n, receive, 0)
        parts = stats[s, :, pl.ds(0, 2 * comps)]
        total = jnp.sum(parts, axis=0) / sp_n
        away = parts - total[None]
        between = jnp.sum(away * away, axis=0) / sp_n
        var = total[comps : 2 * comps] / cols + between[:comps]
        inv = 1.0 / jnp.sqrt(var + epsilon)
        mean = total[:comps]
        i0, i1, i2 = inv[0:1], inv[1:2], inv[2:3]
        a = [chol[pl.ds(i, 1), :] for i in range(7)]
        table = [
            mean[0:1], mean[1:2], mean[2:3],
            a[0] * i0, a[1] * i0, a[2] * i1, a[3] * i0, a[4] * i1, a[5] * i2, a[6],
        ]
        sub = lax.broadcasted_iota(jnp.int32, (16, rows), 0)
        stacked = jnp.zeros((16, rows), jnp.float32)
        for k, v in enumerate(table):
            stacked = jnp.where(sub == k, v, stacked)
        turned = jnp.concatenate([stacked, jnp.zeros((rows - 16, rows), jnp.float32)], axis=0).T
        col = [turned[:, k : k + 1] for k in range(len(table))]
        d0 = filt[s, 0] - col[0]
        d1 = filt[s, 1] - col[1]
        d2 = filt[s, 2] - col[2]
        outbuf[s, 0] = col[9] + col[3] * d0
        outbuf[s, 1] = col[4] * d0 + col[5] * d1
        outbuf[s, 2] = col[6] * d0 + col[7] * d1 + col[8] * d2
        store(s).start()

    def both(s, carry):
        @pl.when(s < steps_n)
        def _():
            span_phase(s)

        @pl.when(s < 2 * FIRST)
        def _():
            first_row_phase(s - FIRST)

        @pl.when(s >= FIRST + LAG)
        def _():
            last_phase(s - LAG)

        @pl.when((s >= FIRST + LAG) & (s < 2 * FIRST + LAG))
        def _():
            last_phase(s - FIRST - LAG)

        return carry

    lax.fori_loop(FIRST, steps_n + LAG, both, 0)

    def finish(s, carry):
        store(s).wait()
        return carry

    lax.fori_loop(0, steps_n, finish, 0)


def body(random_slabs, stress, profile):
    steps_n, comps, rows, cols = random_slabs.shape
    assert rows == 2 * H and cols == 2 * H and comps == 3
    wn_n, sp_n = lax.axis_size("wn"), lax.axis_size("sp")
    f32 = jnp.float32
    half = (steps_n, comps, H, cols)
    return pl.pallas_call(
        functools.partial(kernel, wn_n, sp_n),
        out_shape=jax.ShapeDtypeStruct(random_slabs.shape, f32),
        in_specs=[pl.BlockSpec(memory_space=pltpu.HBM)] * 3,
        out_specs=pl.BlockSpec(memory_space=pl.ANY),
        scratch_shapes=[
            pltpu.VMEM((6, rows), f32),
            pltpu.VMEM((1, rows), f32),
            pltpu.VMEM((steps_n, comps, 2 * rows, cols), f32),
            pltpu.VMEM((steps_n, comps, rows, cols), f32),
            pltpu.VMEM(half, f32),
            pltpu.VMEM(half, f32),
            pltpu.VMEM(half, f32),
            pltpu.VMEM(half, f32),
            pltpu.VMEM((steps_n, comps, rows, cols), f32),
            pltpu.VMEM((steps_n, sp_n, 8, rows), f32),
            pltpu.VMEM((steps_n, comps, rows, cols), f32),
            pltpu.VMEM((rows, 2 * rows), f32),
            pltpu.VMEM((2 * cols, cols), f32),
            pltpu.VMEM((8, rows), f32),
            pltpu.SemaphoreType.DMA((steps_n,)),
            pltpu.SemaphoreType.DMA((2,)),
            pltpu.SemaphoreType.DMA((steps_n,)),
            pltpu.SemaphoreType.DMA((2, steps_n)),
            pltpu.SemaphoreType.DMA((2, steps_n)),
            pltpu.SemaphoreType.DMA((2, steps_n)),
            pltpu.SemaphoreType.DMA((2, steps_n)),
            pltpu.SemaphoreType.DMA((steps_n, sp_n)),
            pltpu.SemaphoreType.DMA((steps_n, sp_n)),
        ],
        compiler_params=pltpu.CompilerParams(
            collective_id=0, has_side_effects=True, vmem_limit_bytes=58 * 2**20
        ),
    )(random_slabs, stress, profile.reshape(1, rows))


def solution(mesh):
    return jax.shard_map(
        body,
        mesh=mesh,
        in_specs=(P(None, None, "wn", "sp"), P(None, "wn"), P("wn")),
        out_specs=P(None, None, "wn", "sp"),
        check_vma=False,
    )
```
